256 devices in a mesh: dp: 32 (over x, z_lo, core), tensor: 8 (over z_hi, y).
Axes of the slice: x: 4, y: 4, z: 8 (z_hi: 2, z_lo: 4; z = z_hi * 4 + z_lo), core: 2. Of those that a mesh axis runs over, the one named last changes fastest.
Arguments:
- pool_rows: bfloat16 [8192, 28672], P('dp', 'tensor'), may hold values from -6 to 6
- out_grads: bfloat16 [131072, 8192], P('dp', 'tensor'), may hold values from -6 to 6
- proj_in: bfloat16 [28672, 64], P('tensor'), may hold values from -0.03125 to 0.03125
- proj_out: bfloat16 [8192, 64], P('tensor'), may hold values from -0.0625 to 0.0625
- token_ids: int32 [131072], P('dp'), may hold values from 0 to 255, as said below
- lengths: int32 [128], P('dp'), may hold values from 256 to 1024, as said below
- queries: bfloat16 [1024, 4096], P('dp', 'tensor'), may hold values from -0.099609375 to 0.099609375
Outputs:
- sketches: float32 [128, 4096], P('dp', 'tensor')
- scores: float32 [128, 1024], P('dp')
The draws below stay inside these ranges and needn't reach their ends.
Inputs may be any that keep to these rules, and one draw needn't show every extreme that they name: `token_ids`: every dp block of 4096 slots uses row 0 and row 255 of its block. `lengths`: the first example of every dp block has all 1024 slots live.
All inputs are finite; a program needn't handle non-finite values.
Results may differ from the reference program's by a relative error of at most 0.0029.
Values may be sent and summed in bfloat16 or wider, within the bound.
A program may use at most 64 MiB of HBM per device.

```python
import jax
import jax.numpy as jnp
from jax import lax

D = 8192
FF = 28672
K = 64
NQ = 1024
LEN = 1024
EX_DEV = 4
POOL_DEV = 256
TOK_DEV = 4096
EXAMPLES = 128
TOKENS = 131072
POOL = 8192


def draw_token_ids(key, part):
    key = jax.random.fold_in(key, 11)
    picked = jax.random.randint(key, (TOKENS,), 0, POOL_DEV, dtype=jnp.int32)
    place = jnp.arange(TOKENS, dtype=jnp.int32) % TOK_DEV
    picked = jnp.where(place == 0, POOL_DEV - 1, picked)
    return jnp.where(place == 1, 0, picked).astype(jnp.int32)


def draw_lengths(key, part):
    key = jax.random.fold_in(key, 12)
    drawn = jax.random.randint(key, (EXAMPLES,), LEN // 4, LEN + 1, dtype=jnp.int32)
    place = jnp.arange(EXAMPLES, dtype=jnp.int32) % EX_DEV
    return jnp.where(place == 0, LEN, drawn).astype(jnp.int32)


def shard_levels(rng, dims, cuts, least, top_value):
    def one(dim, blocks):
        steps = jax.random.uniform(jax.random.fold_in(jax.random.fold_in(rng, 6), dim), (blocks,), jnp.float32, least / len(cuts), top_value / len(cuts))
        return jnp.repeat(jnp.exp(steps), dims[dim] // blocks).reshape((-1,) + (1,) * (len(dims) - dim - 1))

    factor_of = one(*cuts[0])
    for cut in cuts[1:]:
        factor_of = factor_of * one(*cut)
    return factor_of


def bell_draw(stream_key, dims, spread, reach, shards=(), kind=jnp.bfloat16):
    array = spread * jax.random.normal(stream_key, dims, jnp.float32)
    if shards:
        array = array * shard_levels(stream_key, dims, shards, -0.22, 0.18)
    return jnp.clip(array, -reach, reach).astype(kind)


def setup_inputs(seed: int = 0) -> dict:
    streams_of = jax.random.split(jax.random.key(seed), 8)
    pool_rows = bell_draw(streams_of[0], (POOL, FF), 1.0, 6.0, ((0, 32), (1, 8)))
    out_grads = bell_draw(streams_of[1], (TOKENS, D), 1.0, 6.0, ((0, 32), (1, 8)))
    proj_in = bell_draw(streams_of[2], (FF, K), FF ** -0.5, 0.03125, ((0, 8),))
    proj_out = bell_draw(streams_of[3], (D, K), D ** -0.5, 0.0625, ((0, 8),))
    token_ids = draw_token_ids(jax.random.fold_in(streams_of[7], 71), 0)
    lengths = draw_lengths(jax.random.fold_in(streams_of[7], 71), 0)
    queries = bell_draw(streams_of[6], (NQ, K * K), 0.015625, 0.099609375, ((0, 32), (1, 8)))
    return {"pool_rows": pool_rows, "out_grads": out_grads, "proj_in": proj_in, "proj_out": proj_out, "token_ids": token_ids, "lengths": lengths, "queries": queries}


def reference(pool_rows, out_grads, proj_in, proj_out, token_ids, lengths, queries):
    pool_proj = jnp.dot(pool_rows, proj_in, preferred_element_type=jnp.float32)
    grad_proj = jnp.dot(out_grads, proj_out, preferred_element_type=jnp.float32)
    slot = jnp.arange(TOKENS, dtype=jnp.int32)
    rows = token_ids.astype(jnp.int32) + (slot // TOK_DEV).astype(jnp.int32) * POOL_DEV
    in_proj = jnp.take(pool_proj, rows, axis=0)
    place = jnp.arange(LEN, dtype=jnp.int32)
    live = (place[None, :] < lengths[:, None]).astype(jnp.float32)
    weight = live * lax.rsqrt(lengths.astype(jnp.float32))[:, None]
    scaled = grad_proj.reshape(EXAMPLES, LEN, K) * weight[:, :, None]
    sketches = jnp.einsum('tla,tlb->tab', scaled, in_proj.reshape(EXAMPLES, LEN, K), precision=lax.Precision.HIGHEST).reshape(EXAMPLES, K * K)
    sketch_low = sketches.astype(jnp.bfloat16)
    scores = jnp.einsum('ek,qk->eq', sketch_low.astype(jnp.float32), queries.astype(jnp.float32), precision=lax.Precision.HIGHEST)
    return (sketches, scores)
```

```python
import jax
import jax.numpy as jnp
from jax import lax
from jax.experimental import pallas as pl
from jax.experimental.pallas import tpu as pltpu
from jax.sharding import PartitionSpec as P

F32, BF16 = jnp.float32, jnp.bfloat16
MESH = pl.DeviceIdType.MESH
T = 8
NX, NZ, NC = 4, 4, 2


def dot_nt(a, b):
    return lax.dot_general(a, b, (((1,), (1,)), ((), ())), preferred_element_type=F32)


def split(v):
    high = v.astype(BF16)
    return high, (v - high.astype(F32)).astype(BF16)


def kernel(
    pool, grads, pin, pout, ids, lens, qs,
    sk_out, sc_out,
    pool_v, grads_v, pin_v, pout_v, ids_v, lens_v, qall,
    p_send, p_recv, p_tot, s_send, s_recv, sk_v, c_send, c_recv, c_tot,
    in_sem, g_sem, q_local,
    qz_s, qz_r, qx_s, qx_r, qf_s, qf_r, qc_s, qc_r,
    p_s, p_r, a_s, a_r, s_s, s_r, c_s, c_r, d_s, d_r,
):
    me = lax.axis_index("tensor")
    dp = lax.axis_index("dp")
    x, z, c = dp // (NZ * NC), (dp // NC) % NZ, dp % NC
    examples, slots = grads_v.shape[:2]

    loads = [
        pltpu.make_async_copy(s, d, in_sem.at[i])
        for i, (s, d) in enumerate(
            [(pin, pin_v), (pool, pool_v), (pout, pout_v), (ids, ids_v), (lens, lens_v)]
        )
    ]
    for copy in loads:
        copy.start()
    chunks = [
        pltpu.make_async_copy(grads.at[pl.ds(e * slots, slots)], grads_v.at[e], g_sem.at[e])
        for e in range(examples)
    ]
    for copy in chunks:
        copy.start()
    own_q = pltpu.make_async_copy(qs, qall.at[x, z, c], q_local)
    own_q.start()

    def peer(k):
        return lax.rem(me + k, T)

    def source(k):
        return lax.rem(me + T - k, T)

    def device(px, pz, pc):
        return {"dp": (px * NZ + pz) * NC + pc}

    right, left, far = (x + 1) % NX, (x + 3) % NX, (x + 2) % NX
    z_peers = [(z + k) % NZ for k in range(1, NZ)]
    z_sources = [(z + NZ - k) % NZ for k in range(1, NZ)]

    barrier = pltpu.get_barrier_semaphore()
    friends = [{"tensor": peer(k)} for k in range(1, T)]
    friends += [device(x, pz, c) for pz in z_peers]
    friends += [device(right, z, c), device(left, z, c), device(x, z, 1 - c)]
    for friend in friends:
        pl.semaphore_signal(barrier, inc=1, device_id=friend, device_id_type=MESH)
    pl.semaphore_wait(barrier, len(friends))

    def remote(src, dst, send, recv, to):
        return pltpu.make_async_remote_copy(
            src_ref=src, dst_ref=dst, send_sem=send, recv_sem=recv,
            device_id=to, device_id_type=MESH,
        )

    q_z = [
        remote(qs, qall.at[x, z, c], qz_s.at[k], qz_r.at[k], device(x, z_peers[k], c))
        for k in range(NZ - 1)
    ]
    for copy in q_z:
        copy.start()

    loads[0].wait()
    loads[1].wait()
    p_send[...] = dot_nt(pin_v[...], pool_v[...]).reshape(p_send.shape)
    p_out = [
        remote(p_send.at[peer(k)], p_recv.at[me], p_s.at[k], p_r.at[k], {"tensor": peer(k)})
        for k in range(1, T)
    ]
    for copy in p_out:
        copy.start()
    p_recv[me] = p_send[me]

    for copy in loads[2:]:
        copy.wait()
    weights = pout_v[...]
    rows = lax.broadcasted_iota(jnp.int32, (pool_v.shape[0], 128), 0)
    lane = lax.broadcasted_iota(jnp.int32, (1, 128), 1)
    scale = lax.rsqrt(lens_v[...].astype(F32))
    half = 512

    def example(e):
        chunks[e].wait()
        length = lens_v[:, e:e + 1]
        total = None
        for h in range(slots // half):
            grad = dot_nt(weights, grads_v[e, h * half:(h + 1) * half, :])
            pick = []
            for j in range(half // 128):
                first = h * half + j * 128
                row = (e * slots + first) // 128
                token = jnp.where(lane + first < length, ids_v[row:row + 1, :], -1)
                pick.append(jnp.where(rows == token, 1.0, 0.0).astype(BF16))
            part = dot_nt(jnp.concatenate(split(grad), 0), jnp.concatenate(pick, 1))
            total = part if total is None else total + part
        low = total.shape[0] // 2
        total = (total[:low] + total[low:]) * scale[:, e:e + 1]
        s_send[e] = total.reshape(s_send.shape[1:])
        out = [
            remote(s_send.at[e, peer(k)], s_recv.at[e, me], s_s.at[e, k], s_r.at[e, k], {"tensor": peer(k)})
            for k in range(1, T)
        ]
        for copy in out:
            copy.start()
        s_recv[e, me] = s_send[e, me]
        return out

    s_out = [example(0)]

    own_q.wait()
    for copy in q_z:
        copy.wait_recv()
    mine = qall.at[x, :, c]
    q_x = [
        remote(mine, mine, qx_s.at[0], qx_r.at[0], device(right, z, c)),
        remote(mine, mine, qx_s.at[1], qx_r.at[1], device(left, z, c)),
    ]
    other = device(x, z, 1 - c)
    q_c = [remote(mine, mine, qc_s.at[0], qc_r.at[0], other)]
    for copy in q_x + q_c:
        copy.start()

    s_out.append(example(1))

    for copy in p_out:
        copy.wait_recv()
    p_tot[me] = jnp.sum(p_recv[...], axis=0)
    a_out = [
        remote(p_tot.at[me], p_tot.at[me], a_s.at[k], a_r.at[k], {"tensor": peer(k)})
        for k in range(1, T)
    ]
    for copy in a_out:
        copy.start()

    s_out.append(example(2))

    def waiter(dst, send, recv):
        return remote(dst, dst, send, recv, other)

    waiter(qall.at[left, :, c], qx_s.at[0], qx_r.at[0]).wait_recv()
    waiter(qall.at[right, :, c], qx_s.at[1], qx_r.at[1]).wait_recv()
    front, back = qall.at[left, 0:NZ // 2, c], qall.at[right, NZ // 2:NZ, c]
    q_f = [
        remote(front, front, qf_s.at[0], qf_r.at[0], device(right, z, c)),
        remote(back, back, qf_s.at[1], qf_r.at[1], device(left, z, c)),
    ]
    from_left, from_right = qall.at[left, :, c], qall.at[right, :, c]
    q_c += [
        remote(from_left, from_left, qc_s.at[1], qc_r.at[1], other),
        remote(from_right, from_right, qc_s.at[2], qc_r.at[2], other),
    ]
    for copy in q_f + q_c[1:]:
        copy.start()

    s_out.append(example(3))

    waiter(qall.at[far, 0:NZ // 2, c], qf_s.at[0], qf_r.at[0]).wait_recv()
    waiter(qall.at[far, NZ // 2:NZ, c], qf_s.at[1], qf_r.at[1]).wait_recv()
    from_far = qall.at[far, :, c]
    q_c.append(remote(from_far, from_far, qc_s.at[3], qc_r.at[3], other))
    q_c[3].start()

    for copy in a_out:
        copy.wait_recv()
    width = p_tot.shape[0] * p_tot.shape[1]
    p_high, p_low = split(p_tot[...].reshape(width, p_tot.shape[2]))

    totals = []
    for e in range(examples):
        for copy in s_out[e]:
            copy.wait_recv()
        totals.append(jnp.sum(s_recv[e], axis=0))
    t_high, t_low = split(jnp.concatenate(totals, 0))
    n = t_high.shape[0]
    both = dot_nt(jnp.concatenate([t_high, t_low], 0), p_high)
    sk_v[...] = both[:n] + both[n:] + dot_nt(t_high, p_low)
    share = s_recv.shape[2]
    flat = jnp.concatenate([sk_v[pl.ds(a, examples, stride=share), :] for a in range(share)], 1)
    sk_out[...] = flat

    waiter(qall.at[x, :, 1 - c], qc_s.at[0], qc_r.at[0]).wait_recv()
    waiter(qall.at[left, :, 1 - c], qc_s.at[1], qc_r.at[1]).wait_recv()
    waiter(qall.at[right, :, 1 - c], qc_s.at[2], qc_r.at[2]).wait_recv()
    waiter(qall.at[far, :, 1 - c], qc_s.at[3], qc_r.at[3]).wait_recv()
    queries = qall[...].reshape(T * 128, flat.shape[1])
    part = dot_nt(flat.astype(BF16), queries)
    for t in range(T):
        c_send[t] = part[:, t * 128:(t + 1) * 128]
    c_out = [
        remote(c_send.at[peer(k)], c_recv.at[me], c_s.at[k], c_r.at[k], {"tensor": peer(k)})
        for k in range(1, T)
    ]
    for copy in c_out:
        copy.start()
    c_recv[me] = c_send[me]
    for copy in c_out:
        copy.wait_recv()
    c_tot[me] = jnp.sum(c_recv[...], axis=0)
    d_out = [
        remote(c_tot.at[me], c_tot.at[me], d_s.at[k], d_r.at[k], {"tensor": peer(k)})
        for k in range(1, T)
    ]
    for copy in d_out:
        copy.start()
    for copy in d_out:
        copy.wait_recv()
    for t in range(T):
        sc_out[:, t * 128:(t + 1) * 128] = c_tot[t]

    for copy in q_z + q_x + q_f + q_c + p_out + a_out + sum(s_out, []) + c_out + d_out:
        copy.wait_send()


def local(pool_rows, out_grads, proj_in, proj_out, token_ids, lengths, queries):
    examples = lengths.shape[0]
    slots = out_grads.shape[0] // examples
    width = proj_in.shape[1]
    share = width // T
    pool = pool_rows.shape[0]
    model = out_grads.shape[1]
    rows, cols = queries.shape
    any_spec = pl.BlockSpec(memory_space=pltpu.HBM)
    dma = pltpu.SemaphoreType.DMA
    vmem = pltpu.VMEM
    return pl.pallas_call(
        kernel,
        out_shape=(
            jax.ShapeDtypeStruct((examples, share * width), F32),
            jax.ShapeDtypeStruct((examples, rows * NX * NZ * NC), F32),
        ),
        in_specs=[any_spec] * 7,
        out_specs=[pl.BlockSpec(memory_space=pltpu.VMEM)] * 2,
        scratch_shapes=[
            vmem(pool_rows.shape, BF16),
            vmem((examples, slots, model), BF16),
            vmem(proj_in.shape[::-1], BF16),
            vmem(proj_out.shape[::-1], BF16),
            vmem((token_ids.shape[0] // 128, 128), jnp.int32),
            vmem((1, examples), jnp.int32),
            vmem((NX, NZ, NC, rows, cols), BF16),
            vmem((T, share, pool), F32),
            vmem((T, share, pool), F32),
            vmem((T, share, pool), F32),
            vmem((examples, T, share, pool), F32),
            vmem((examples, T, share, pool), F32),
            vmem((examples * share, width), F32),
            vmem((T, examples, 128), F32),
            vmem((T, examples, 128), F32),
            vmem((T, examples, 128), F32),
            dma((5,)), dma((examples,)), dma(()),
            dma((3,)), dma((3,)), dma((2,)), dma((2,)), dma((2,)), dma((2,)), dma((4,)), dma((4,)),
            dma((T,)), dma((T,)), dma((T,)), dma((T,)),
            dma((examples, T)), dma((examples, T)),
            dma((T,)), dma((T,)), dma((T,)), dma((T,)),
        ],
        compiler_params=pltpu.CompilerParams(
            collective_id=0, has_side_effects=True, vmem_limit_bytes=48 * 1024 * 1024
        ),
    )(
        pool_rows, out_grads, proj_in.T, proj_out.T,
        token_ids.reshape(-1, 128), lengths.reshape(1, -1), queries,
    )


def solution(mesh):
    return jax.shard_map(
        local,
        mesh=mesh,
        in_specs=(
            P("dp", "tensor"),
            P("dp", "tensor"),
            P("tensor", None),
            P("tensor", None),
            P("dp"),
            P("dp"),
            P("dp", "tensor"),
        ),
        out_specs=(P("dp", "tensor"), P("dp", None)),
        check_vma=False,
    )
```

```python
import jax
import jax.numpy as jnp
from jax import lax
from jax.experimental import pallas as pl
from jax.experimental.pallas import tpu as pltpu
from jax.sharding import PartitionSpec as P

F32, BF16 = jnp.float32, jnp.bfloat16
MESH = pl.DeviceIdType.MESH
T = 8
NY = 4
NX, NZ, NC = 4, 4, 2


def dot_nt(a, b):
    return lax.dot_general(a, b, (((1,), (1,)), ((), ())), preferred_element_type=F32)


def split(v):
    high = v.astype(BF16)
    return high, (v - high.astype(F32)).astype(BF16)


def kernel(
    pool, grads, pin, pout, ids, lens, qs,
    sk_out, sc_out,
    pool_v, grads_v, pin_v, pout_v, ids_v, lens_v, qall, pick_v, cat_v,
    p_send, p_recv, p_part, s_send, s_recv, z_send, z_recv, sk_v, c_send, c_recv,
    in_sem, g_sem, q_local,
    qz_s, qz_r, qx_s, qx_r, qc_s, qc_r,
    p_s, p_r, a_s, a_r, s_s, s_r, z_s, z_r, c_s, c_r,
):
    me = lax.axis_index("tensor")
    dp = lax.axis_index("dp")
    zh, y = me // NY, me % NY
    x, z, c = dp // (NZ * NC), (dp // NC) % NZ, dp % NC
    examples, slots = grads_v.shape[:2]

    loads = [
        pltpu.make_async_copy(s, d, in_sem.at[i])
        for i, (s, d) in enumerate(
            [(ids, ids_v), (lens, lens_v), (pin, pin_v), (pool, pool_v), (pout, pout_v)]
        )
    ]
    for copy in loads:
        copy.start()
    chunks = [
        pltpu.make_async_copy(grads.at[pl.ds(e * slots, slots)], grads_v.at[e], g_sem.at[e])
        for e in range(examples)
    ]
    for copy in chunks:
        copy.start()
    own_q = pltpu.make_async_copy(qs, qall.at[x, z, c], q_local)
    own_q.start()

    def device(px, pz, pc):
        return {"dp": (px * NZ + pz) * NC + pc}

    def peer(k):
        return lax.rem(me + k, T)

    y_to = [(y + k) % NY for k in range(1, NY)]
    z_to = [(z + k) % NZ for k in range(1, NZ)]
    z_from = [(z + NZ - k) % NZ for k in range(1, NZ)]
    x_to = [(x + k) % NX for k in range(1, NX)]
    x_from = [(x + NX - k) % NX for k in range(1, NX)]
    other = device(x, z, 1 - c)
    partner = {"tensor": (1 - zh) * NY + y}

    barrier = pltpu.get_barrier_semaphore()
    friends = [partner, other]
    friends += [{"tensor": zh * NY + p} for p in y_to]
    friends += [device(x, p, c) for p in z_to]
    friends += [device(p, z, c) for p in x_to]
    for friend in friends:
        pl.semaphore_signal(barrier, inc=1, device_id=friend, device_id_type=MESH)

    def remote(src, dst, send, recv, to):
        return pltpu.make_async_remote_copy(
            src_ref=src, dst_ref=dst, send_sem=send, recv_sem=recv,
            device_id=to, device_id_type=MESH,
        )

    def start(copies):
        for copy in copies:
            copy.start()
        sent.extend(copies)

    sent = []

    for copy in loads[:4]:
        copy.wait()
    p_send[...] = dot_nt(pin_v[...], pool_v[...]).reshape(p_send.shape)
    rows = lax.broadcasted_iota(jnp.int32, (pool_v.shape[0], 128), 0)
    lane = lax.broadcasted_iota(jnp.int32, (1, 128), 1)
    scale = lax.rsqrt(lens_v[...].astype(F32))
    for e in range(examples):
        length = lens_v[:, e:e + 1]
        for first in range(0, slots, 128):
            row = (e * slots + first) // 128
            token = jnp.where(lane + first < length, ids_v[row:row + 1, :], -1)
            pick_v[e, :, first:first + 128] = jnp.where(rows == token, 1.0, 0.0).astype(BF16)
    loads[4].wait()

    def project(e):
        chunks[e].wait()
        high, low = split(dot_nt(pout_v[...], grads_v[e]))
        n = high.shape[0]
        cat_v[e % 2, :n, :] = high
        cat_v[e % 2, n:, :] = low

    def gather(e):
        both = dot_nt(cat_v[e % 2], pick_v[e])
        n = both.shape[0] // 2
        total = ((both[:n] + both[n:]) * scale[:, e:e + 1]).astype(BF16)
        share = n // T
        for p in range(NY):
            s_send[p, e, :share] = total[p * share:(p + 1) * share]
            s_send[p, e, share:] = total[n // 2 + p * share:n // 2 + (p + 1) * share]

    project(0)
    project(1)
    gather(0)

    pl.semaphore_wait(barrier, len(friends))
    p_out = [
        remote(p_send.at[p], p_recv.at[y], p_s.at[k], p_r.at[k], {"tensor": zh * NY + p})
        for k, p in enumerate(y_to)
    ]
    start(p_out)
    q_z = [
        remote(qs, qall.at[x, z, c], qz_s.at[k], qz_r.at[k], device(x, p, c))
        for k, p in enumerate(z_to)
    ]
    start(q_z)

    def along_x(step, pz):
        block = qall.at[x, pz, c]
        return [
            remote(block, block, qx_s.at[k, step], qx_r.at[k, step], device(p, z, c))
            for k, p in enumerate(x_to)
        ]

    own_q.wait()
    start(along_x(0, z))

    project(2)
    gather(1)
    project(3)
    gather(2)
    gather(3)
    s_out = [
        remote(s_send.at[p], s_recv.at[y], s_s.at[k], s_r.at[k], {"tensor": zh * NY + p})
        for k, p in enumerate(y_to)
    ]
    start(s_out)

    p_recv[y] = p_send[y]
    for copy in p_out:
        copy.wait_recv()
    p_part[me] = jnp.sum(p_recv[...], axis=0)
    a_out = [
        remote(p_part.at[me], p_part.at[me], a_s.at[k - 1], a_r.at[k - 1], {"tensor": peer(k)})
        for k in range(1, T)
    ]
    start(a_out)

    for k in range(NZ - 1):
        remote(qs, qall.at[x, z_from[k], c], qz_s.at[k], qz_r.at[k], other).wait_recv()
        start(along_x(k + 1, z_from[k]))

    def across(k, px):
        line = qall.at[px, :, c]
        return remote(line, line, qc_s.at[k], qc_r.at[k], other)

    start([across(0, x)])

    s_recv[y] = s_send[y]
    for copy in s_out:
        copy.wait_recv()
    over_y = s_recv[0].astype(F32)
    for p in range(1, NY):
        over_y = over_y + s_recv[p].astype(F32)
    z_send[...] = over_y.reshape(z_send.shape)
    z_out = remote(z_send.at[:, 1 - zh], z_recv, z_s, z_r, partner)
    start([z_out])

    for k in range(NX - 1):
        for step in range(NZ):
            pz = z if step == 0 else z_from[step - 1]
            block = qall.at[x_from[k], pz, c]
            remote(block, block, qx_s.at[k, step], qx_r.at[k, step], other).wait_recv()
        start([across(k + 1, x_from[k])])

    for copy in a_out:
        copy.wait_recv()
    p_all = p_part[0:NY] + p_part[NY:T]
    p_high, p_low = split(p_all.reshape(NY * p_all.shape[1], p_all.shape[2]))

    z_out.wait_recv()
    mine = z_send[:, zh] + z_recv[...]
    share = mine.shape[1]
    t_high, t_low = split(mine.reshape(examples * share, mine.shape[2]))
    n = t_high.shape[0]
    both = dot_nt(jnp.concatenate([t_high, t_low], 0), p_high)
    sk_v[...] = both[:n] + both[n:] + dot_nt(t_high, p_low)
    flat = jnp.concatenate([sk_v[pl.ds(a, examples, stride=share), :] for a in range(share)], 1)
    sk_out[...] = flat

    for k in range(NX):
        px = x if k == 0 else x_from[k - 1]
        line = qall.at[px, :, 1 - c]
        remote(line, line, qc_s.at[k], qc_r.at[k], other).wait_recv()
    queries = qall[...].reshape(-1, flat.shape[1])
    part = dot_nt(jnp.concatenate(split(flat), 0), queries)
    c_send[...] = part[:examples] + part[examples:]
    c_out = [
        remote(c_send, c_recv.at[me], c_s.at[k - 1], c_r.at[k - 1], {"tensor": peer(k)})
        for k in range(1, T)
    ]
    start(c_out)
    c_recv[me] = c_send[...]
    for copy in c_out:
        copy.wait_recv()
    sc_out[...] = jnp.sum(c_recv[...], axis=0)

    for copy in sent:
        copy.wait_send()


def finish(a, b, a_out, b_out, sems):
    copies = [pltpu.make_async_copy(a, a_out, sems.at[0]), pltpu.make_async_copy(b, b_out, sems.at[1])]
    for copy in copies:
        copy.start()
    for copy in copies:
        copy.wait()


def local(pool_rows, out_grads, proj_in, proj_out, token_ids, lengths, queries):
    examples = lengths.shape[0]
    slots = out_grads.shape[0] // examples
    width = proj_in.shape[1]
    share = width // T
    pool = pool_rows.shape[0]
    model = out_grads.shape[1]
    rows, cols = queries.shape
    any_spec = pl.BlockSpec(memory_space=pl.ANY)
    dma = pltpu.SemaphoreType.DMA
    vmem = pltpu.VMEM
    sketches, scores = pl.pallas_call(
        kernel,
        out_shape=(
            jax.ShapeDtypeStruct((examples, share * width), F32),
            jax.ShapeDtypeStruct((examples, rows * NX * NZ * NC), F32),
        ),
        in_specs=[any_spec] * 7,
        out_specs=[pl.BlockSpec(memory_space=pltpu.VMEM)] * 2,
        scratch_shapes=[
            vmem(pool_rows.shape, BF16),
            vmem((examples, slots, model), BF16),
            vmem(proj_in.shape[::-1], BF16),
            vmem(proj_out.shape[::-1], BF16),
            vmem((token_ids.shape[0] // 128, 128), jnp.int32),
            vmem((1, examples), jnp.int32),
            vmem((NX, NZ, NC, rows, cols), BF16),
            vmem((examples, pool, slots), BF16),
            vmem((2, 2 * width, slots), BF16),
            vmem((NY, width // NY, pool), F32),
            vmem((NY, width // NY, pool), F32),
            vmem((T, width // NY, pool), F32),
            vmem((NY, examples, 2 * share, pool), BF16),
            vmem((NY, examples, 2 * share, pool), BF16),
            vmem((examples, 2, share, pool), F32),
            vmem((examples, share, pool), F32),
            vmem((examples * share, width), F32),
            vmem((examples, rows * NX * NZ * NC), F32),
            vmem((T, examples, rows * NX * NZ * NC), F32),
            dma((5,)), dma((examples,)), dma(()),
            dma((3,)), dma((3,)), dma((3, NZ)), dma((3, NZ)), dma((NX,)), dma((NX,)),
            dma((3,)), dma((3,)), dma((T - 1,)), dma((T - 1,)),
            dma((3,)), dma((3,)), dma(()), dma(()), dma((T - 1,)), dma((T - 1,)),
        ],
        compiler_params=pltpu.CompilerParams(
            collective_id=0, has_side_effects=True, vmem_limit_bytes=60 * 1024 * 1024
        ),
    )(
        pool_rows, out_grads, proj_in.T, proj_out.T,
        token_ids.reshape(-1, 128), lengths.reshape(1, -1), queries,
    )
    return pl.pallas_call(
        finish,
        out_shape=(
            jax.ShapeDtypeStruct(sketches.shape, F32),
            jax.ShapeDtypeStruct(scores.shape, F32),
        ),
        in_specs=[any_spec] * 2,
        out_specs=[any_spec] * 2,
        scratch_shapes=[dma((2,))],
        compiler_params=pltpu.CompilerParams(vmem_limit_bytes=60 * 1024 * 1024),
    )(sketches, scores)


def solution(mesh):
    return jax.shard_map(
        local,
        mesh=mesh,
        in_specs=(
            P("dp", "tensor"),
            P("dp", "tensor"),
            P("tensor", None),
            P("tensor", None),
            P("dp"),
            P("dp"),
            P("dp", "tensor"),
        ),
        out_specs=(P("dp", "tensor"), P("dp", None)),
        check_vma=False,
    )
```

```python
import jax
import jax.numpy as jnp
from jax import lax
from jax.experimental import pallas as pl
from jax.experimental.pallas import tpu as pltpu
from jax.sharding import PartitionSpec as P

F32, BF16 = jnp.float32, jnp.bfloat16
MESH = pl.DeviceIdType.MESH
T = 8
NY = 4
GATES = 3, 0
NX, NZ, NC = 4, 4, 2


def dot_nt(a, b):
    return lax.dot_general(a, b, (((1,), (1,)), ((), ())), preferred_element_type=F32)


def split(v):
    high = v.astype(BF16)
    return high, (v - high.astype(F32)).astype(BF16)


def kernel(
    pool, grads, pin, pout, ids, lens, qs,
    sk_out, sc_out,
    pool_v, grads_v, pin_v, pout_v, ids_v, lens_v, qall, pick_v, cat_v,
    p_send, p_recv, p_part, s_send, s_recv, z_send, z_recv, sk_v, c_send, c_recv,
    in_sem, g_sem, q_local,
    qz_s, qz_r, qx_s, qx_r, qc_s, qc_r,
    p_s, p_r, a_s, a_r, s_s, s_r, z_s, z_r, c_s, c_r,
):
    me = lax.axis_index("tensor")
    dp = lax.axis_index("dp")
    zh, y = me // NY, me % NY
    x, z, c = dp // (NZ * NC), (dp // NC) % NZ, dp % NC
    examples, slots = grads_v.shape[:2]

    def device(px, pz, pc):
        return {"dp": (px * NZ + pz) * NC + pc}

    def peer(k):
        return lax.rem(me + k, T)

    y_to = [(y + k) % NY for k in range(1, NY)]
    z_to = [(z + k) % NZ for k in range(1, NZ)]
    z_from = [(z + NZ - k) % NZ for k in range(1, NZ)]
    x_to = [(x + k) % NX for k in range(1, NX)]
    x_from = [(x + NX - k) % NX for k in range(1, NX)]
    other = device(x, z, 1 - c)
    partner = {"tensor": (1 - zh) * NY + y}

    barrier = pltpu.get_barrier_semaphore()
    friends = [partner, other]
    friends += [{"tensor": zh * NY + p} for p in y_to]
    friends += [device(x, p, c) for p in z_to]
    friends += [device(p, z, c) for p in x_to]
    for friend in friends:
        pl.semaphore_signal(barrier, inc=1, device_id=friend, device_id_type=MESH)

    loads = [
        pltpu.make_async_copy(s, d, in_sem.at[i])
        for i, (s, d) in enumerate(
            [(ids, ids_v), (lens, lens_v), (pin, pin_v), (pool, pool_v), (pout, pout_v)]
        )
    ]
    for copy in loads:
        copy.start()
    chunks = [
        pltpu.make_async_copy(grads.at[pl.ds(e * slots, slots)], grads_v.at[e], g_sem.at[e])
        for e in range(examples)
    ]
    for copy in chunks:
        copy.start()
    own_q = pltpu.make_async_copy(qs, qall.at[x, z, c], q_local)
    own_q.start()

    def remote(src, dst, send, recv, to):
        return pltpu.make_async_remote_copy(
            src_ref=src, dst_ref=dst, send_sem=send, recv_sem=recv,
            device_id=to, device_id_type=MESH,
        )

    def start(copies):
        for copy in copies:
            copy.start()
        sent.extend(copies)

    sent = []

    loads[0].wait()
    loads[1].wait()
    rows = lax.broadcasted_iota(jnp.int32, (pool_v.shape[0], 128), 0)
    lane = lax.broadcasted_iota(jnp.int32, (1, 128), 1)
    scale = lax.rsqrt(lens_v[...].astype(F32))
    for e in range(examples):
        length = lens_v[:, e:e + 1]
        for first in range(0, slots, 128):
            row = (e * slots + first) // 128
            token = jnp.where(lane + first < length, ids_v[row:row + 1, :], -1)
            pick_v[e, :, first:first + 128] = jnp.where(rows == token, 1.0, 0.0).astype(BF16)

    def project(e):
        high, low = split(dot_nt(pout_v[...], grads_v[e]))
        n = high.shape[0]
        cat_v[e, :n, :] = high
        cat_v[e, n:, :] = low

    def gather(e):
        both = dot_nt(cat_v[e], pick_v[e])
        n = both.shape[0] // 2
        total = ((both[:n] + both[n:]) * scale[:, e:e + 1]).astype(BF16)
        share = n // T
        for p in range(NY):
            s_send[p, e, :share] = total[p * share:(p + 1) * share]
            s_send[p, e, share:] = total[n // 2 + p * share:n // 2 + (p + 1) * share]

    p_out = [
        remote(p_send.at[p], p_recv.at[y], p_s.at[k], p_r.at[k], {"tensor": zh * NY + p})
        for k, p in enumerate(y_to)
    ]
    q_z = [
        remote(qs, qall.at[x, z, c], qz_s.at[k], qz_r.at[k], device(x, p, c))
        for k, p in enumerate(z_to)
    ]

    def along_x(step, pz, block):
        return [
            remote(block, qall.at[x, pz, c], qx_s.at[k, step], qx_r.at[k, step], device(p, z, c))
            for k, p in enumerate(x_to)
        ]

    q_x = along_x(0, z, qs)
    sent.extend(p_out + q_z + q_x)

    def gate():
        pl.semaphore_wait(barrier, len(friends))
        for copy in p_out + q_z + q_x:
            copy.start()

    def gate_at(place):
        if GATES[0] == place and GATES[1] == place:
            gate()
        elif GATES[0] == place:
            pl.when(zh == 0)(gate)
        elif GATES[1] == place:
            pl.when(zh != 0)(gate)

    for copy in loads[2:]:
        copy.wait()
    p_send[...] = dot_nt(pin_v[...], pool_v[...]).reshape(p_send.shape)
    gate_at(0)
    chunks[0].wait()
    project(0)
    gate_at(1)
    chunks[1].wait()
    project(1)
    gather(0)
    gate_at(2)
    chunks[2].wait()
    chunks[3].wait()
    project(2)
    gather(1)
    project(3)
    gather(2)
    gather(3)
    gate_at(3)
    s_out = [
        remote(s_send.at[p], s_recv.at[y], s_s.at[k], s_r.at[k], {"tensor": zh * NY + p})
        for k, p in enumerate(y_to)
    ]
    start(s_out)

    p_recv[y] = p_send[y]
    for copy in p_out:
        copy.wait_recv()
    p_part[me] = jnp.sum(p_recv[...], axis=0)
    a_out = [
        remote(p_part.at[me], p_part.at[me], a_s.at[k - 1], a_r.at[k - 1], {"tensor": peer(k)})
        for k in range(1, T)
    ]
    start(a_out)

    for k in range(NZ - 1):
        remote(qs, qall.at[x, z_from[k], c], qz_s.at[k], qz_r.at[k], other).wait_recv()
        start(along_x(k + 1, z_from[k], qall.at[x, z_from[k], c]))

    def across(k, px):
        line = qall.at[px, :, c]
        return remote(line, line, qc_s.at[k], qc_r.at[k], other)

    own_q.wait()
    start([across(0, x)])

    s_recv[y] = s_send[y]
    for copy in s_out:
        copy.wait_recv()
    over_y = s_recv[0].astype(F32)
    for p in range(1, NY):
        over_y = over_y + s_recv[p].astype(F32)
    z_send[...] = over_y.reshape(z_send.shape)
    z_out = remote(z_send.at[:, 1 - zh], z_recv, z_s, z_r, partner)
    start([z_out])

    for k in range(NX - 1):
        for step in range(NZ):
            pz = z if step == 0 else z_from[step - 1]
            block = qall.at[x_from[k], pz, c]
            remote(block, block, qx_s.at[k, step], qx_r.at[k, step], other).wait_recv()
        start([across(k + 1, x_from[k])])

    for copy in a_out:
        copy.wait_recv()
    p_all = p_part[0:NY] + p_part[NY:T]
    p_high, p_low = split(p_all.reshape(NY * p_all.shape[1], p_all.shape[2]))

    z_out.wait_recv()
    mine = z_send[:, zh] + z_recv[...]
    share = mine.shape[1]
    t_high, t_low = split(mine.reshape(examples * share, mine.shape[2]))
    n = t_high.shape[0]
    both = dot_nt(jnp.concatenate([t_high, t_low], 0), p_high)
    sk_v[...] = both[:n] + both[n:] + dot_nt(t_high, p_low)
    flat = jnp.concatenate([sk_v[pl.ds(a, examples, stride=share), :] for a in range(share)], 1)
    sk_out[...] = flat

    for k in range(NX):
        px = x if k == 0 else x_from[k - 1]
        line = qall.at[px, :, 1 - c]
        remote(line, line, qc_s.at[k], qc_r.at[k], other).wait_recv()
    queries = qall[...].reshape(-1, flat.shape[1])
    part = dot_nt(jnp.concatenate(split(flat), 0), queries)
    c_send[...] = part[:examples] + part[examples:]
    c_out = [
        remote(c_send, c_recv.at[me], c_s.at[k - 1], c_r.at[k - 1], {"tensor": peer(k)})
        for k in range(1, T)
    ]
    start(c_out)
    c_recv[me] = c_send[...]
    for copy in c_out:
        copy.wait_recv()
    sc_out[...] = jnp.sum(c_recv[...], axis=0)

    for copy in sent:
        copy.wait_send()


def local(pool_rows, out_grads, proj_in, proj_out, token_ids, lengths, queries):
    examples = lengths.shape[0]
    slots = out_grads.shape[0] // examples
    width = proj_in.shape[1]
    share = width // T
    pool = pool_rows.shape[0]
    model = out_grads.shape[1]
    rows, cols = queries.shape
    any_spec = pl.BlockSpec(memory_space=pl.ANY)
    dma = pltpu.SemaphoreType.DMA
    vmem = pltpu.VMEM
    return pl.pallas_call(
        kernel,
        out_shape=(
            vmem((examples, share * width), F32),
            vmem((examples, rows * NX * NZ * NC), F32),
        ),
        in_specs=[any_spec] * 7,
        out_specs=[pl.BlockSpec(memory_space=pltpu.VMEM)] * 2,
        scratch_shapes=[
            vmem(pool_rows.shape, BF16),
            vmem((examples, slots, model), BF16),
            vmem(proj_in.shape[::-1], BF16),
            vmem(proj_out.shape[::-1], BF16),
            vmem((token_ids.shape[0] // 128, 128), jnp.int32),
            vmem((1, examples), jnp.int32),
            vmem((NX, NZ, NC, rows, cols), BF16),
            vmem((examples, pool, slots), BF16),
            vmem((examples, 2 * width, slots), BF16),
            vmem((NY, width // NY, pool), F32),
            vmem((NY, width // NY, pool), F32),
            vmem((T, width // NY, pool), F32),
            vmem((NY, examples, 2 * share, pool), BF16),
            vmem((NY, examples, 2 * share, pool), BF16),
            vmem((examples, 2, share, pool), F32),
            vmem((examples, share, pool), F32),
            vmem((examples * share, width), F32),
            vmem((examples, rows * NX * NZ * NC), F32),
            vmem((T, examples, rows * NX * NZ * NC), F32),
            dma((5,)), dma((examples,)), dma(()),
            dma((3,)), dma((3,)), dma((3, NZ)), dma((3, NZ)), dma((NX,)), dma((NX,)),
            dma((3,)), dma((3,)), dma((T - 1,)), dma((T - 1,)),
            dma((3,)), dma((3,)), dma(()), dma(()), dma((T - 1,)), dma((T - 1,)),
        ],
        compiler_params=pltpu.CompilerParams(
            collective_id=0, has_side_effects=True, vmem_limit_bytes=60 * 1024 * 1024
        ),
    )(
        pool_rows, out_grads, proj_in.T, proj_out.T,
        token_ids.reshape(-1, 128), lengths.reshape(1, -1), queries,
    )


def solution(mesh):
    return jax.shard_map(
        local,
        mesh=mesh,
        in_specs=(
            P("dp", "tensor"),
            P("dp", "tensor"),
            P("tensor", None),
            P("tensor", None),
            P("dp"),
            P("dp"),
            P("dp", "tensor"),
        ),
        out_specs=(P("dp", "tensor"), P("dp", None)),
        check_vma=False,
    )
```

```python
import jax
import jax.numpy as jnp
from jax import lax
from jax.experimental import pallas as pl
from jax.experimental.pallas import tpu as pltpu
from jax.sharding import PartitionSpec as P

F32, BF16 = jnp.float32, jnp.bfloat16
MESH = pl.DeviceIdType.MESH
T = 8
NY = 4
GATES = 3, 0
FAR = 2, 1, 3, 0, 2, 1, 3
NX, NZ, NC = 4, 4, 2


def dot_nt(a, b):
    return lax.dot_general(a, b, (((1,), (1,)), ((), ())), preferred_element_type=F32)


def split(v):
    high = v.astype(BF16)
    return high, (v - high.astype(F32)).astype(BF16)


def kernel(
    pool, grads, pin, pout, ids, lens, qs,
    sk_out, sc_out,
    pool_v, grads_v, pin_v, pout_v, ids_v, lens_v, qall, pick_v, cat_v,
    p_send, p_recv, p_part, s_send, s_recv, z_send, z_recv, sk_v, c_send, c_recv,
    in_sem, g_sem, q_local,
    qz_s, qz_r, qx_s, qx_r, qc_s, qc_r,
    p_s, p_r, a_s, a_r, s_s, s_r, z_s, z_r, c_s, c_r,
):
    me = lax.axis_index("tensor")
    dp = lax.axis_index("dp")
    zh, y = me // NY, me % NY
    x, z, c = dp // (NZ * NC), (dp // NC) % NZ, dp % NC
    examples, slots = grads_v.shape[:2]

    def device(px, pz, pc):
        return {"dp": (px * NZ + pz) * NC + pc}

    def peer(k):
        half = (1 - zh) if k < NY else zh
        return half * NY + (y + FAR[k]) % NY

    y_to = [(y + k) % NY for k in range(1, NY)]
    z_near = [z + 1 - 2 * (z % 2), 2 - z // 2, 3 - 3 * (z // 2)]
    x_to = [(x + k) % NX for k in (2, 1, 3)]
    x_from = [(x + NX - k) % NX for k in (2, 1, 3)]
    other = device(x, z, 1 - c)
    partner = {"tensor": (1 - zh) * NY + y}

    barrier = pltpu.get_barrier_semaphore()
    friends = [partner, other]
    friends += [{"tensor": zh * NY + p} for p in y_to]
    friends += [device(x, p, c) for p in z_near]
    friends += [device(p, z, c) for p in x_to]
    for friend in friends:
        pl.semaphore_signal(barrier, inc=1, device_id=friend, device_id_type=MESH)

    loads = [
        pltpu.make_async_copy(s, d, in_sem.at[i])
        for i, (s, d) in enumerate(
            [(ids, ids_v), (lens, lens_v), (pin, pin_v), (pool, pool_v), (pout, pout_v)]
        )
    ]
    for copy in loads:
        copy.start()
    chunks = [
        pltpu.make_async_copy(grads.at[pl.ds(e * slots, slots)], grads_v.at[e], g_sem.at[e])
        for e in range(examples)
    ]
    for copy in chunks:
        copy.start()
    own_q = pltpu.make_async_copy(qs, qall.at[x, z, c], q_local)
    own_q.start()

    def remote(src, dst, send, recv, to):
        return pltpu.make_async_remote_copy(
            src_ref=src, dst_ref=dst, send_sem=send, recv_sem=recv,
            device_id=to, device_id_type=MESH,
        )

    def start(copies):
        for copy in copies:
            copy.start()
        sent.extend(copies)

    sent = []

    loads[0].wait()
    loads[1].wait()
    rows = lax.broadcasted_iota(jnp.int32, (pool_v.shape[0], 128), 0)
    lane = lax.broadcasted_iota(jnp.int32, (1, 128), 1)
    scale = lax.rsqrt(lens_v[...].astype(F32))
    for e in range(examples):
        length = lens_v[:, e:e + 1]
        for first in range(0, slots, 128):
            row = (e * slots + first) // 128
            token = jnp.where(lane + first < length, ids_v[row:row + 1, :], -1)
            pick_v[e, :, first:first + 128] = jnp.where(rows == token, 1.0, 0.0).astype(BF16)

    def project(e):
        high, low = split(dot_nt(pout_v[...], grads_v[e]))
        n = high.shape[0]
        cat_v[e, :n, :] = high
        cat_v[e, n:, :] = low

    def gather(e):
        both = dot_nt(cat_v[e], pick_v[e])
        n = both.shape[0] // 2
        total = ((both[:n] + both[n:]) * scale[:, e:e + 1]).astype(BF16)
        share = n // T
        for p in range(NY):
            s_send[p, e, :share] = total[p * share:(p + 1) * share]
            s_send[p, e, share:] = total[n // 2 + p * share:n // 2 + (p + 1) * share]

    p_out = [
        remote(p_send.at[p], p_recv.at[y], p_s.at[k], p_r.at[k], {"tensor": zh * NY + p})
        for k, p in enumerate(y_to)
    ]
    q_z = [
        remote(qs, qall.at[x, z, c], qz_s.at[k], qz_r.at[z], device(x, z_near[k], c))
        for k in (2, 1, 0)
    ]

    def along_x(pz, block):
        return [
            remote(block, qall.at[x, pz, c], qx_s.at[k, pz], qx_r.at[k, pz], device(p, z, c))
            for k, p in enumerate(x_to)
        ]

    q_x = along_x(z, qs)
    q_on = [along_x(z_near[k], qall.at[x, z_near[k], c]) for k in range(NZ - 1)]
    sent.extend(p_out + q_z + q_x + sum(q_on, []))

    def pass_on(k):
        block = qall.at[x, z_near[k], c]
        remote(block, block, qz_s.at[k], qz_r.at[z_near[k]], other).wait_recv()
        for copy in q_on[k]:
            copy.start()

    def gate():
        pl.semaphore_wait(barrier, len(friends))
        for copy in p_out + q_z + q_x:
            copy.start()

    def gate_at(place):
        if GATES[0] == place and GATES[1] == place:
            gate()
        elif GATES[0] == place:
            pl.when(zh == 0)(gate)
        elif GATES[1] == place:
            pl.when(zh != 0)(gate)

    for copy in loads[2:]:
        copy.wait()
    p_send[...] = dot_nt(pin_v[...], pool_v[...]).reshape(p_send.shape)
    gate_at(0)
    chunks[0].wait()
    project(0)
    gate_at(1)
    chunks[1].wait()
    project(1)
    gather(0)
    gate_at(2)
    chunks[2].wait()
    chunks[3].wait()
    project(2)
    gather(1)
    pl.when(zh != 0)(lambda: pass_on(0))
    project(3)
    gather(2)
    gather(3)
    gate_at(3)
    s_out = [
        remote(s_send.at[p], s_recv.at[y], s_s.at[k], s_r.at[k], {"tensor": zh * NY + p})
        for k, p in enumerate(y_to)
    ]
    start(s_out)

    pl.when(zh == 0)(lambda: pass_on(0))

    p_recv[y] = p_send[y]
    for copy in p_out:
        copy.wait_recv()
    p_part[me] = jnp.sum(p_recv[...], axis=0)
    a_out = [
        remote(p_part.at[me], p_part.at[me], a_s.at[k], a_r.at[k], {"tensor": peer(k)})
        for k in range(T - 1)
    ]
    start(a_out)

    pass_on(1)
    pass_on(2)

    def across(px, pz):
        block = qall.at[px, pz, c]
        copy = remote(block, block, qc_s.at[px, pz], qc_r.at[px, pz], other)
        copy.start()
        return copy

    def arrived(k, pz):
        block = qall.at[x_from[k], pz, c]
        remote(block, block, qx_s.at[k, pz], qx_r.at[k, pz], other).wait_recv()
        return across(x_from[k], pz)

    own_q.wait()
    sent += [across(x, z)] + [across(x, pz) for pz in z_near]
    sent += [arrived(k, z) for k in (1, 2, 0)]

    s_recv[y] = s_send[y]
    for copy in s_out:
        copy.wait_recv()
    over_y = s_recv[0].astype(F32)
    for p in range(1, NY):
        over_y = over_y + s_recv[p].astype(F32)
    z_send[...] = over_y.reshape(z_send.shape)
    z_out = remote(z_send.at[:, 1 - zh], z_recv, z_s, z_r, partner)
    start([z_out])

    for pz in z_near:
        sent += [arrived(k, pz) for k in (1, 2, 0)]

    for copy in a_out:
        copy.wait_recv()
    p_all = p_part[0:NY] + p_part[NY:T]
    p_high, p_low = split(p_all.reshape(NY * p_all.shape[1], p_all.shape[2]))
    p_cat = jnp.concatenate([p_high, p_high, p_low], 1)

    z_out.wait_recv()
    mine = z_send[:, zh] + z_recv[...]
    share = mine.shape[1]
    t_high, t_low = split(mine.reshape(examples * share, mine.shape[2]))
    sk_v[...] = dot_nt(jnp.concatenate([t_high, t_low, t_high], 1), p_cat)
    flat = jnp.concatenate([sk_v[pl.ds(a, examples, stride=share), :] for a in range(share)], 1)
    sk_out[...] = flat

    for pz in [z] + z_near:
        for px in [x] + x_from:
            block = qall.at[px, pz, 1 - c]
            remote(block, block, qc_s.at[px, pz], qc_r.at[px, pz], other).wait_recv()
    queries = qall[...].reshape(-1, flat.shape[1])
    part = dot_nt(jnp.concatenate(split(flat), 0), queries)
    c_send[...] = part[:examples] + part[examples:]
    c_out = [
        remote(c_send, c_recv.at[me], c_s.at[k], c_r.at[k], {"tensor": peer(k)})
        for k in range(T - 1)
    ]
    start(c_out)
    c_recv[me] = c_send[...]
    for copy in c_out:
        copy.wait_recv()
    sc_out[...] = jnp.sum(c_recv[...], axis=0)

    for copy in sent:
        copy.wait_send()


def local(pool_rows, out_grads, proj_in, proj_out, token_ids, lengths, queries):
    examples = lengths.shape[0]
    slots = out_grads.shape[0] // examples
    width = proj_in.shape[1]
    share = width // T
    pool = pool_rows.shape[0]
    model = out_grads.shape[1]
    rows, cols = queries.shape
    any_spec = pl.BlockSpec(memory_space=pl.ANY)
    dma = pltpu.SemaphoreType.DMA
    vmem = pltpu.VMEM
    return pl.pallas_call(
        kernel,
        out_shape=(
            vmem((examples, share * width), F32),
            vmem((examples, rows * NX * NZ * NC), F32),
        ),
        in_specs=[any_spec] * 7,
        out_specs=[pl.BlockSpec(memory_space=pltpu.VMEM)] * 2,
        scratch_shapes=[
            vmem(pool_rows.shape, BF16),
            vmem((examples, slots, model), BF16),
            vmem(proj_in.shape[::-1], BF16),
            vmem(proj_out.shape[::-1], BF16),
            vmem((token_ids.shape[0] // 128, 128), jnp.int32),
            vmem((1, examples), jnp.int32),
            vmem((NX, NZ, NC, rows, cols), BF16),
            vmem((examples, pool, slots), BF16),
            vmem((examples, 2 * width, slots), BF16),
            vmem((NY, width // NY, pool), F32),
            vmem((NY, width // NY, pool), F32),
            vmem((T, width // NY, pool), F32),
            vmem((NY, examples, 2 * share, pool), BF16),
            vmem((NY, examples, 2 * share, pool), BF16),
            vmem((examples, 2, share, pool), F32),
            vmem((examples, share, pool), F32),
            vmem((examples * share, width), F32),
            vmem((examples, rows * NX * NZ * NC), F32),
            vmem((T, examples, rows * NX * NZ * NC), F32),
            dma((5,)), dma((examples,)), dma(()),
            dma((3,)), dma((NZ,)), dma((3, NZ)), dma((3, NZ)), dma((NX, NZ)), dma((NX, NZ)),
            dma((3,)), dma((3,)), dma((T - 1,)), dma((T - 1,)),
            dma((3,)), dma((3,)), dma(()), dma(()), dma((T - 1,)), dma((T - 1,)),
        ],
        compiler_params=pltpu.CompilerParams(
            collective_id=0, has_side_effects=True, vmem_limit_bytes=60 * 1024 * 1024
        ),
    )(
        pool_rows, out_grads, proj_in.T, proj_out.T,
        token_ids.reshape(-1, 128), lengths.reshape(1, -1), queries,
    )


def solution(mesh):
    return jax.shard_map(
        local,
        mesh=mesh,
        in_specs=(
            P("dp", "tensor"),
            P("dp", "tensor"),
            P("tensor", None),
            P("tensor", None),
            P("dp"),
            P("dp"),
            P("dp", "tensor"),
        ),
        out_specs=(P("dp", "tensor"), P("dp", None)),
        check_vma=False,
    )
```

```python
import jax
import jax.numpy as jnp
from jax import lax
from jax.experimental import pallas as pl
from jax.experimental.pallas import tpu as pltpu
from jax.sharding import PartitionSpec as P

F32, BF16 = jnp.float32, jnp.bfloat16
MESH = pl.DeviceIdType.MESH
T = 8
NY = 4
GATES = 3, 0
FAR = 2, 1, 3, 0, 2, 1, 3
NX, NZ, NC = 4, 4, 2


def dot_nt(a, b):
    return lax.dot_general(a, b, (((1,), (1,)), ((), ())), preferred_element_type=F32)


def split(v):
    high = v.astype(BF16)
    return high, (v - high.astype(F32)).astype(BF16)


def kernel(
    pool, grads, pin, pout, ids, lens, qs,
    sk_out, sc_out,
    pool_v, grads_v, pin_v, pout_v, ids_v, lens_v, qall, pick_v, cat_v,
    p_send, p_recv, p_part, s_send, s_recv, z_send, z_recv, sk_v, c_send, c_recv,
    in_sem, g_sem, q_local,
    qz_s, qz_r, qx_s, qx_r, qc_s, qc_r,
    p_s, p_r, a_s, a_r, s_s, s_r, z_s, z_r, c_s, c_r,
):
    me = lax.axis_index("tensor")
    dp = lax.axis_index("dp")
    zh, y = me // NY, me % NY
    x, z, c = dp // (NZ * NC), (dp // NC) % NZ, dp % NC
    examples, slots = grads_v.shape[:2]

    def device(px, pz, pc):
        return {"dp": (px * NZ + pz) * NC + pc}

    def peer(k):
        half = (1 - zh) if k < NY else zh
        return half * NY + (y + FAR[k]) % NY

    y_to = [(y + k) % NY for k in range(1, NY)]
    z_near = [z + 1 - 2 * (z % 2), 2 - z // 2, 3 - 3 * (z // 2)]
    x_to = [(x + k) % NX for k in (2, 1, 3)]
    x_from = [(x + NX - k) % NX for k in (2, 1, 3)]
    other = device(x, z, 1 - c)
    partner = {"tensor": (1 - zh) * NY + y}

    barrier = pltpu.get_barrier_semaphore()
    friends = [partner, other]
    friends += [{"tensor": zh * NY + p} for p in y_to]
    friends += [device(x, p, c) for p in z_near]
    friends += [device(p, z, c) for p in x_to]
    for friend in friends:
        pl.semaphore_signal(barrier, inc=1, device_id=friend, device_id_type=MESH)

    loads = [
        pltpu.make_async_copy(s, d, in_sem.at[i])
        for i, (s, d) in enumerate(
            [(ids, ids_v), (lens, lens_v), (pin, pin_v), (pool, pool_v), (pout, pout_v)]
        )
    ]
    for copy in loads:
        copy.start()
    chunks = [
        pltpu.make_async_copy(grads.at[pl.ds(e * slots, slots)], grads_v.at[e], g_sem.at[e])
        for e in range(examples)
    ]
    for copy in chunks:
        copy.start()
    own_q = pltpu.make_async_copy(qs, qall.at[x, z, c], q_local)
    own_q.start()

    def remote(src, dst, send, recv, to):
        return pltpu.make_async_remote_copy(
            src_ref=src, dst_ref=dst, send_sem=send, recv_sem=recv,
            device_id=to, device_id_type=MESH,
        )

    def start(copies):
        for copy in copies:
            copy.start()
        sent.extend(copies)

    sent = []

    loads[0].wait()
    loads[1].wait()
    rows = lax.broadcasted_iota(jnp.int32, (pool_v.shape[0], 128), 0)
    lane = lax.broadcasted_iota(jnp.int32, (1, 128), 1)
    scale = lax.rsqrt(lens_v[...].astype(F32))
    for e in range(examples):
        length = lens_v[:, e:e + 1]
        for first in range(0, slots, 128):
            row = (e * slots + first) // 128
            token = jnp.where(lane + first < length, ids_v[row:row + 1, :], -1)
            pick_v[e, :, first:first + 128] = jnp.where(rows == token, 1.0, 0.0).astype(BF16)

    def project(e):
        high, low = split(dot_nt(pout_v[...], grads_v[e]))
        n = high.shape[0]
        cat_v[e, :n, :] = high
        cat_v[e, n:, :] = low

    def gather(e):
        both = dot_nt(cat_v[e], pick_v[e])
        n = both.shape[0] // 2
        total = (both[:n] + both[n:]) * scale[:, e:e + 1]
        share = n // T
        for p in range(NY):
            low, high = p * share, n // 2 + p * share
            pair = jnp.concatenate([total[low:low + share], total[high:high + share]], 0)
            s_send[p, e] = pair.astype(BF16)

    p_out = [
        remote(p_send.at[p], p_recv.at[y], p_s.at[k], p_r.at[k], {"tensor": zh * NY + p})
        for k, p in enumerate(y_to)
    ]
    q_z = [
        remote(qs, qall.at[x, z, c], qz_s.at[k], qz_r.at[z], device(x, z_near[k], c))
        for k in (2, 1, 0)
    ]

    def along_x(pz, block):
        return [
            remote(block, qall.at[x, pz, c], qx_s.at[k, pz], qx_r.at[k, pz], device(p, z, c))
            for k, p in enumerate(x_to)
        ]

    q_x = along_x(z, qs)
    q_on = [along_x(z_near[k], qall.at[x, z_near[k], c]) for k in range(NZ - 1)]
    sent.extend(p_out + q_z + q_x + sum(q_on, []))

    def pass_on(k):
        block = qall.at[x, z_near[k], c]
        remote(block, block, qz_s.at[k], qz_r.at[z_near[k]], other).wait_recv()
        for copy in q_on[k]:
            copy.start()

    def gate():
        pl.semaphore_wait(barrier, len(friends))
        for copy in p_out + q_z + q_x:
            copy.start()

    def gate_at(place):
        if GATES[0] == place and GATES[1] == place:
            gate()
        elif GATES[0] == place:
            pl.when(zh == 0)(gate)
        elif GATES[1] == place:
            pl.when(zh != 0)(gate)

    for copy in loads[2:]:
        copy.wait()
    p_send[...] = dot_nt(pin_v[...], pool_v[...]).reshape(p_send.shape)
    gate_at(0)
    chunks[0].wait()
    project(0)
    gate_at(1)
    chunks[1].wait()
    project(1)
    gather(0)
    gate_at(2)
    chunks[2].wait()
    chunks[3].wait()
    project(2)
    gather(1)
    pl.when(zh != 0)(lambda: pass_on(0))
    project(3)
    gather(2)
    gather(3)
    gate_at(3)
    s_out = [
        remote(s_send.at[p], s_recv.at[y], s_s.at[k], s_r.at[k], {"tensor": zh * NY + p})
        for k, p in enumerate(y_to)
    ]
    start(s_out)

    pl.when(zh == 0)(lambda: pass_on(0))

    p_recv[y] = p_send[y]
    for copy in p_out:
        copy.wait_recv()
    p_part[me] = jnp.sum(p_recv[...], axis=0)
    a_out = [
        remote(p_part.at[me], p_part.at[me], a_s.at[k], a_r.at[k], {"tensor": peer(k)})
        for k in range(T - 1)
    ]
    start(a_out)

    pass_on(1)
    pass_on(2)

    def across(px, pz):
        block = qall.at[px, pz, c]
        copy = remote(block, block, qc_s.at[px, pz], qc_r.at[px, pz], other)
        copy.start()
        return copy

    def arrived(k, pz):
        block = qall.at[x_from[k], pz, c]
        remote(block, block, qx_s.at[k, pz], qx_r.at[k, pz], other).wait_recv()
        return across(x_from[k], pz)

    own_q.wait()
    sent += [across(x, z)] + [across(x, pz) for pz in z_near]
    sent += [arrived(k, z) for k in (1, 2, 0)]

    s_recv[y] = s_send[y]
    for copy in s_out:
        copy.wait_recv()
    over_y = s_recv[0].astype(F32)
    for p in range(1, NY):
        over_y = over_y + s_recv[p].astype(F32)
    z_send[...] = over_y.reshape(z_send.shape)
    z_out = remote(z_send.at[:, 1 - zh], z_recv, z_s, z_r, partner)
    start([z_out])

    for pz in z_near:
        sent += [arrived(k, pz) for k in (1, 2, 0)]

    for copy in a_out:
        copy.wait_recv()
    p_all = p_part[0:NY] + p_part[NY:T]
    p_high, p_low = split(p_all.reshape(NY * p_all.shape[1], p_all.shape[2]))
    p_cat = jnp.concatenate([p_high, p_high, p_low], 1)

    z_out.wait_recv()
    mine = z_send[:, zh] + z_recv[...]
    share = mine.shape[1]
    t_high, t_low = split(mine.reshape(examples * share, mine.shape[2]))
    sk_v[...] = dot_nt(jnp.concatenate([t_high, t_low, t_high], 1), p_cat)
    flat = jnp.concatenate([sk_v[pl.ds(a, examples, stride=share), :] for a in range(share)], 1)
    sk_out[...] = flat

    for pz in [z] + z_near:
        for px in [x] + x_from:
            block = qall.at[px, pz, 1 - c]
            remote(block, block, qc_s.at[px, pz], qc_r.at[px, pz], other).wait_recv()
    queries = qall[...].reshape(-1, flat.shape[1])
    part = dot_nt(jnp.concatenate(split(flat), 0), queries)
    c_send[...] = part[:examples] + part[examples:]
    c_out = [
        remote(c_send, c_recv.at[me], c_s.at[k], c_r.at[k], {"tensor": peer(k)})
        for k in range(T - 1)
    ]
    start(c_out)
    c_recv[me] = c_send[...]
    for copy in c_out:
        copy.wait_recv()
    sc_out[...] = jnp.sum(c_recv[...], axis=0)

    for copy in sent:
        copy.wait_send()


def local(pool_rows, out_grads, proj_in, proj_out, token_ids, lengths, queries):
    examples = lengths.shape[0]
    slots = out_grads.shape[0] // examples
    width = proj_in.shape[1]
    share = width // T
    pool = pool_rows.shape[0]
    model = out_grads.shape[1]
    rows, cols = queries.shape
    any_spec = pl.BlockSpec(memory_space=pl.ANY)
    dma = pltpu.SemaphoreType.DMA
    vmem = pltpu.VMEM
    return pl.pallas_call(
        kernel,
        out_shape=(
            vmem((examples, share * width), F32),
            vmem((examples, rows * NX * NZ * NC), F32),
        ),
        in_specs=[any_spec] * 7,
        out_specs=[pl.BlockSpec(memory_space=pltpu.VMEM)] * 2,
        scratch_shapes=[
            vmem(pool_rows.shape, BF16),
            vmem((examples, slots, model), BF16),
            vmem(proj_in.shape[::-1], BF16),
            vmem(proj_out.shape[::-1], BF16),
            vmem((token_ids.shape[0] // 128, 128), jnp.int32),
            vmem((1, examples), jnp.int32),
            vmem((NX, NZ, NC, rows, cols), BF16),
            vmem((examples, pool, slots), BF16),
            vmem((examples, 2 * width, slots), BF16),
            vmem((NY, width // NY, pool), F32),
            vmem((NY, width // NY, pool), F32),
            vmem((T, width // NY, pool), F32),
            vmem((NY, examples, 2 * share, pool), BF16),
            vmem((NY, examples, 2 * share, pool), BF16),
            vmem((examples, 2, share, pool), F32),
            vmem((examples, share, pool), F32),
            vmem((examples * share, width), F32),
            vmem((examples, rows * NX * NZ * NC), F32),
            vmem((T, examples, rows * NX * NZ * NC), F32),
            dma((5,)), dma((examples,)), dma(()),
            dma((3,)), dma((NZ,)), dma((3, NZ)), dma((3, NZ)), dma((NX, NZ)), dma((NX, NZ)),
            dma((3,)), dma((3,)), dma((T - 1,)), dma((T - 1,)),
            dma((3,)), dma((3,)), dma(()), dma(()), dma((T - 1,)), dma((T - 1,)),
        ],
        compiler_params=pltpu.CompilerParams(
            collective_id=0, has_side_effects=True, vmem_limit_bytes=60 * 1024 * 1024
        ),
    )(
        pool_rows, out_grads, proj_in.T, proj_out.T,
        token_ids.reshape(-1, 128), lengths.reshape(1, -1), queries,
    )


def solution(mesh):
    return jax.shard_map(
        local,
        mesh=mesh,
        in_specs=(
            P("dp", "tensor"),
            P("dp", "tensor"),
            P("tensor", None),
            P("tensor", None),
            P("dp"),
            P("dp"),
            P("dp", "tensor"),
        ),
        out_specs=(P("dp", "tensor"), P("dp", None)),
        check_vma=False,
    )
```

```python
import jax
import jax.numpy as jnp
from jax import lax
from jax.experimental import pallas as pl
from jax.experimental.pallas import tpu as pltpu
from jax.sharding import PartitionSpec as P

F32, BF16 = jnp.float32, jnp.bfloat16
MESH = pl.DeviceIdType.MESH
T = 8
NY = 4
GATES = 3, 0
FAR = 2, 1, 3, 0, 2, 1, 3
NX, NZ, NC = 4, 4, 2


def dot_nt(a, b):
    return lax.dot_general(a, b, (((1,), (1,)), ((), ())), preferred_element_type=F32)


def split(v):
    high = v.astype(BF16)
    return high, (v - high.astype(F32)).astype(BF16)


def kernel(
    pool, grads, pin, pout, ids, lens, qs,
    sk_out, sc_out,
    pool_v, grads_v, pin_v, pout_v, ids_v, lens_v, qall, pick_v, cat_v,
    p_send, p_recv, p_part, s_send, s_recv, z_send, z_recv, sk_v, c_send, c_recv,
    in_sem, g_sem, q_local,
    qz_s, qz_r, qx_s, qx_r, qc_s, qc_r,
    p_s, p_r, a_s, a_r, s_s, s_r, z_s, z_r, c_s, c_r,
):
    me = lax.axis_index("tensor")
    dp = lax.axis_index("dp")
    zh, y = me // NY, me % NY
    x, z, c = dp // (NZ * NC), (dp // NC) % NZ, dp % NC
    examples, slots = grads_v.shape[:2]

    def device(px, pz, pc):
        return {"dp": (px * NZ + pz) * NC + pc}

    def peer(k):
        half = (1 - zh) if k < NY else zh
        return half * NY + (y + FAR[k]) % NY

    y_to = [(y + k) % NY for k in range(1, NY)]
    z_near = [z + 1 - 2 * (z % 2), 2 - z // 2, 3 - 3 * (z // 2)]
    x_to = [(x + k) % NX for k in (2, 1, 3)]
    x_from = [(x + NX - k) % NX for k in (2, 1, 3)]
    other = device(x, z, 1 - c)
    partner = {"tensor": (1 - zh) * NY + y}

    barrier = pltpu.get_barrier_semaphore()
    friends = [partner]
    friends += [device(p, z, c) for p in x_to]
    friends += [{"tensor": zh * NY + (y + k) % NY} for k in (2, 1, 3)]
    friends += [device(x, p, c) for p in z_near[::-1]] + [other]
    for friend in friends:
        pl.semaphore_signal(barrier, inc=1, device_id=friend, device_id_type=MESH)

    loads = [
        pltpu.make_async_copy(s, d, in_sem.at[i])
        for i, (s, d) in enumerate(
            [(ids, ids_v), (lens, lens_v), (pin, pin_v), (pool, pool_v), (pout, pout_v)]
        )
    ]
    for copy in loads:
        copy.start()
    chunks = [
        pltpu.make_async_copy(grads.at[pl.ds(e * slots, slots)], grads_v.at[e], g_sem.at[e])
        for e in range(examples)
    ]
    for copy in chunks:
        copy.start()
    own_q = pltpu.make_async_copy(qs, qall.at[x, z, c], q_local)
    own_q.start()

    def remote(src, dst, send, recv, to):
        return pltpu.make_async_remote_copy(
            src_ref=src, dst_ref=dst, send_sem=send, recv_sem=recv,
            device_id=to, device_id_type=MESH,
        )

    def start(copies):
        for copy in copies:
            copy.start()
        sent.extend(copies)

    sent = []

    loads[0].wait()
    loads[1].wait()
    rows = lax.broadcasted_iota(jnp.int32, (pool_v.shape[0], 128), 0)
    lane = lax.broadcasted_iota(jnp.int32, (1, 128), 1)
    scale = lax.rsqrt(lens_v[...].astype(F32))
    for e in range(examples):
        length = lens_v[:, e:e + 1]
        for first in range(0, slots, 128):
            row = (e * slots + first) // 128
            token = jnp.where(lane + first < length, ids_v[row:row + 1, :], -1)
            pick_v[e, :, first:first + 128] = jnp.where(rows == token, 1.0, 0.0).astype(BF16)

    def project(e):
        high, low = split(dot_nt(pout_v[...], grads_v[e]))
        n = high.shape[0]
        cat_v[e, :n, :] = high
        cat_v[e, n:, :] = low

    def gather(e):
        both = dot_nt(cat_v[e], pick_v[e])
        n = both.shape[0] // 2
        total = (both[:n] + both[n:]) * scale[:, e:e + 1]
        share = n // T
        for p in range(NY):
            low, high = p * share, n // 2 + p * share
            pair = jnp.concatenate([total[low:low + share], total[high:high + share]], 0)
            s_send[p, e] = pair

    p_out = [
        remote(p_send.at[p], p_recv.at[y], p_s.at[k], p_r.at[k], {"tensor": zh * NY + p})
        for k, p in enumerate(y_to)
    ]
    q_z = [
        remote(qs, qall.at[x, z, c], qz_s.at[k], qz_r.at[z], device(x, z_near[k], c))
        for k in (2, 1, 0)
    ]

    def along_x(pz, block):
        return [
            remote(block, qall.at[x, pz, c], qx_s.at[k, pz], qx_r.at[k, pz], device(p, z, c))
            for k, p in enumerate(x_to)
        ]

    q_x = along_x(z, qs)
    q_on = [along_x(z_near[k], qall.at[x, z_near[k], c]) for k in range(NZ - 1)]
    sent.extend(p_out + q_z + q_x + sum(q_on, []))

    def pass_on(k):
        block = qall.at[x, z_near[k], c]
        remote(block, block, qz_s.at[k], qz_r.at[z_near[k]], other).wait_recv()
        for copy in q_on[k]:
            copy.start()

    def gate():
        pl.semaphore_wait(barrier, len(friends))
        for copy in p_out + q_z + q_x:
            copy.start()

    def gate_at(place):
        if GATES[0] == place and GATES[1] == place:
            gate()
        elif GATES[0] == place:
            pl.when(zh == 0)(gate)
        elif GATES[1] == place:
            pl.when(zh != 0)(gate)

    for copy in loads[2:]:
        copy.wait()
    p_send[...] = dot_nt(pin_v[...], pool_v[...]).reshape(p_send.shape)
    gate_at(0)
    chunks[0].wait()
    project(0)
    gate_at(1)
    chunks[1].wait()
    project(1)
    gather(0)
    gate_at(2)
    chunks[2].wait()
    chunks[3].wait()
    project(2)
    gather(1)
    pl.when(zh != 0)(lambda: pass_on(0))
    project(3)
    gather(2)
    gather(3)
    gate_at(3)
    s_out = [
        remote(s_send.at[p], s_recv.at[y], s_s.at[k], s_r.at[k], {"tensor": zh * NY + p})
        for k, p in enumerate(y_to)
    ]
    start(s_out)

    pl.when(zh == 0)(lambda: pass_on(0))

    p_recv[y] = p_send[y]
    for copy in p_out:
        copy.wait_recv()
    p_part[me] = jnp.sum(p_recv[...], axis=0)
    a_out = [
        remote(p_part.at[me], p_part.at[me], a_s.at[k], a_r.at[k], {"tensor": peer(k)})
        for k in range(T - 1)
    ]
    start(a_out)

    pass_on(1)
    pass_on(2)

    def across(px, pz):
        block = qall.at[px, pz, c]
        copy = remote(block, block, qc_s.at[px, pz], qc_r.at[px, pz], other)
        copy.start()
        return copy

    def arrived(k, pz):
        block = qall.at[x_from[k], pz, c]
        remote(block, block, qx_s.at[k, pz], qx_r.at[k, pz], other).wait_recv()
        return across(x_from[k], pz)

    own_q.wait()
    sent += [across(x, z)] + [across(x, pz) for pz in z_near]
    sent += [arrived(k, z) for k in (1, 2, 0)]

    s_recv[y] = s_send[y]
    for copy in s_out:
        copy.wait_recv()
    over_y = jnp.sum(s_recv[...], axis=0)
    z_send[...] = over_y.reshape(z_send.shape)
    z_out = remote(z_send.at[:, 1 - zh], z_recv, z_s, z_r, partner)
    start([z_out])

    for pz in z_near:
        sent += [arrived(k, pz) for k in (1, 2, 0)]

    for copy in a_out:
        copy.wait_recv()
    p_all = p_part[0:NY] + p_part[NY:T]
    p_high, p_low = split(p_all.reshape(NY * p_all.shape[1], p_all.shape[2]))
    p_cat = jnp.concatenate([p_high, p_high, p_low], 1)

    z_out.wait_recv()
    mine = z_send[:, zh] + z_recv[...]
    share = mine.shape[1]
    t_high, t_low = split(mine.reshape(examples * share, mine.shape[2]))
    sk_v[...] = dot_nt(jnp.concatenate([t_high, t_low, t_high], 1), p_cat)
    flat = jnp.concatenate([sk_v[pl.ds(a, examples, stride=share), :] for a in range(share)], 1)
    sk_out[...] = flat

    for pz in [z] + z_near:
        for px in [x] + x_from:
            block = qall.at[px, pz, 1 - c]
            remote(block, block, qc_s.at[px, pz], qc_r.at[px, pz], other).wait_recv()
    queries = qall[...].reshape(-1, flat.shape[1])
    part = dot_nt(jnp.concatenate(split(flat), 0), queries)
    c_send[...] = part[:examples] + part[examples:]
    c_out = [
        remote(c_send, c_recv.at[me], c_s.at[k], c_r.at[k], {"tensor": peer(k)})
        for k in range(T - 1)
    ]
    start(c_out)
    c_recv[me] = c_send[...]
    for copy in c_out:
        copy.wait_recv()
    sc_out[...] = jnp.sum(c_recv[...], axis=0)

    for copy in sent:
        copy.wait_send()


def local(pool_rows, out_grads, proj_in, proj_out, token_ids, lengths, queries):
    examples = lengths.shape[0]
    slots = out_grads.shape[0] // examples
    width = proj_in.shape[1]
    share = width // T
    pool = pool_rows.shape[0]
    model = out_grads.shape[1]
    rows, cols = queries.shape
    any_spec = pl.BlockSpec(memory_space=pl.ANY)
    dma = pltpu.SemaphoreType.DMA
    vmem = pltpu.VMEM
    return pl.pallas_call(
        kernel,
        out_shape=(
            vmem((examples, share * width), F32),
            vmem((examples, rows * NX * NZ * NC), F32),
        ),
        in_specs=[any_spec] * 7,
        out_specs=[pl.BlockSpec(memory_space=pltpu.VMEM)] * 2,
        scratch_shapes=[
            vmem(pool_rows.shape, BF16),
            vmem((examples, slots, model), BF16),
            vmem(proj_in.shape[::-1], BF16),
            vmem(proj_out.shape[::-1], BF16),
            vmem((token_ids.shape[0] // 128, 128), jnp.int32),
            vmem((1, examples), jnp.int32),
            vmem((NX, NZ, NC, rows, cols), BF16),
            vmem((examples, pool, slots), BF16),
            vmem((examples, 2 * width, slots), BF16),
            vmem((NY, width // NY, pool), F32),
            vmem((NY, width // NY, pool), F32),
            vmem((T, width // NY, pool), F32),
            vmem((NY, examples, 2 * share, pool), F32),
            vmem((NY, examples, 2 * share, pool), F32),
            vmem((examples, 2, share, pool), F32),
            vmem((examples, share, pool), F32),
            vmem((examples * share, width), F32),
            vmem((examples, rows * NX * NZ * NC), F32),
            vmem((T, examples, rows * NX * NZ * NC), F32),
            dma((5,)), dma((examples,)), dma(()),
            dma((3,)), dma((NZ,)), dma((3, NZ)), dma((3, NZ)), dma((NX, NZ)), dma((NX, NZ)),
            dma((3,)), dma((3,)), dma((T - 1,)), dma((T - 1,)),
            dma((3,)), dma((3,)), dma(()), dma(()), dma((T - 1,)), dma((T - 1,)),
        ],
        compiler_params=pltpu.CompilerParams(
            collective_id=0, has_side_effects=True, vmem_limit_bytes=60 * 1024 * 1024
        ),
    )(
        pool_rows, out_grads, proj_in.T, proj_out.T,
        token_ids.reshape(-1, 128), lengths.reshape(1, -1), queries,
    )


def solution(mesh):
    return jax.shard_map(
        local,
        mesh=mesh,
        in_specs=(
            P("dp", "tensor"),
            P("dp", "tensor"),
            P("tensor", None),
            P("tensor", None),
            P("dp"),
            P("dp"),
            P("dp", "tensor"),
        ),
        out_specs=(P("dp", "tensor"), P("dp", None)),
        check_vma=False,
    )
```
